256 devices in a mesh: rows: 4 (over y), cols: 64 (over x, z, core).
Axes of the slice: x: 4, y: 4, z: 8, core: 2. Of those that a mesh axis runs over, the one named last changes fastest.
Arguments:
- sensitivity: bfloat16 [4, 256, 512, 512], P('rows', 'cols'), may hold values from -0.25 to 0.25
- tile_rows: int32 [4, 256], P('rows', 'cols'), may hold values from 0 to 127, as said below
- tile_cols: int32 [4, 256], P('rows', 'cols'), may hold values from 0 to 1, as said below
- kept_counts: int32 [4, 256], P('rows', 'cols'), may hold values from 0 to 512, as said below
- misfit: float32 [262144], P('rows'), may hold values from -6 to 6
- data_weight: float32 [262144], P('rows'), may hold values from 0.3 to 3
- depth_weight: float32 [65536], P('cols'), may hold values from 0.25 to 3
- density: float32 [65536], P('cols'), may hold values from -6 to 6
Outputs:
- new_density: float32 [65536], P('cols')
- new_misfit: float32 [262144], P(('rows', 'cols'))
The draws below stay inside these ranges and needn't reach their ends.
Inputs may be any that keep to these rules, and one draw needn't show every extreme that they name: Within the 4 slots of one device the pairs (tile_rows, tile_cols) are distinct. Within the 4 slots of one device the pairs (tile_rows, tile_cols) are distinct. A slot with kept_counts 0 is empty, and empty slots come after all live slots of a device; a live slot keeps 512 // 2 or more coefficients; every device has a live slot, and some device has all 4 slots live.
All inputs are finite; a program needn't handle non-finite values.
Results may differ from the reference program's by a relative error of at most 0.033.
Values may be sent and summed in bfloat16 or wider, within the bound.
No kernel may reach another device: no remote copies, remote signals or barrier semaphores. Data moves between devices by JAX's collectives and lax.ppermute only.
A program may use at most 64 MiB of HBM per device.

```python
import math
import jax
import jax.numpy as jnp
from jax import lax

TB = 512
DB = 128
MB = 2
SLOTS = 4
ITERS = 4
NDATA = 262144
NCELL = 65536
N_ROWS = 4
N_COLS = 64


def pattern_all(key):
    base_key = jax.random.fold_in(key, 7001)
    device_total = N_ROWS * N_COLS
    key_order, key_live, key_full, key_kept = jax.random.split(base_key, 4)
    device_keys = jax.random.split(key_order, device_total)

    def single(device_key):
        return jax.random.permutation(device_key, DB * MB)[:SLOTS].astype(jnp.int32)
    positions = jax.vmap(single)(device_keys)
    live_total = jax.random.randint(key_live, (device_total,), 1, max(2, SLOTS // 2) + 1)
    heavy_devices = jax.random.permutation(key_full, device_total)[:max(1, device_total // 32)]
    full_device = jnp.zeros((device_total,), jnp.int32).at[heavy_devices].set(1)
    live_total = jnp.where(full_device > 0, SLOTS, live_total)
    slot_index = jnp.arange(SLOTS, dtype=jnp.int32)[None, :]
    kept_draw = jax.random.randint(key_kept, (device_total, SLOTS), TB // 2, TB + 1)
    kept_draw = jnp.where(slot_index == 0, TB, kept_draw)
    kept_values = jnp.where(slot_index < live_total[:, None], kept_draw, 0).astype(jnp.int32)
    rows_values = (positions // MB).astype(jnp.int32)
    cols_values = (positions % MB).astype(jnp.int32)
    shaped = lambda values: values.reshape(N_ROWS, N_COLS * SLOTS)
    return (shaped(rows_values), shaped(cols_values), shaped(kept_values))


def draw_tile_rows(key, part):
    return pattern_all(key)[0]


def draw_tile_cols(key, part):
    return pattern_all(key)[1]


def draw_kept_counts(key, part):
    return pattern_all(key)[2]


def draw_depth_weight(key, part):
    position = jnp.arange(NCELL, dtype=jnp.float32) / NCELL
    trend = 0.5 * jnp.exp(position * jnp.log(3.0))
    roughness = jnp.exp(jax.random.uniform(key, (NCELL,), jnp.float32, jnp.log(0.5), jnp.log(2.0)))
    return (trend * roughness).astype(jnp.float32)


def level_of(own_key, dims, shards, low, high):
    gain, own = 1.0, jax.random.fold_in(own_key, 6)
    for dim, blocks in shards:
        draws = jnp.exp(jax.random.uniform(jax.random.fold_in(own, dim), (blocks,), jnp.float32, low / len(shards), high / len(shards)))
        gain = gain * jnp.repeat(draws, dims[dim] // blocks).reshape([-1 if axis == dim else 1 for axis in range(len(dims))])
    return gain


def bell_draw(rng, shape, width, bound, cuts=(), held_as=jnp.bfloat16):
    factor_of = level_of(rng, shape, cuts, -0.22, 0.18) if cuts else 1.0
    result = jax.random.normal(rng, shape, jnp.float32) * width * factor_of
    return jnp.minimum(jnp.maximum(result, -bound), bound).astype(held_as)


def setup_inputs(seed: int = 0) -> dict:
    splits = jax.random.split(jax.random.key(seed), 9)
    sensitivity = bell_draw(splits[0], (N_ROWS, N_COLS * SLOTS, TB, TB), TB ** -0.5, 0.25, ((0, 4), (1, 64)))
    tile_rows = draw_tile_rows(jax.random.fold_in(splits[8], 71), 0)
    tile_cols = draw_tile_cols(jax.random.fold_in(splits[8], 71), 0)
    kept_counts = draw_kept_counts(jax.random.fold_in(splits[8], 71), 0)
    misfit = bell_draw(splits[4], (NDATA,), 1.0, 6.0, ((0, 4),), jnp.float32)
    data_weight = jnp.clip(jnp.exp(math.log(3.0) - 2.3025851 * jax.random.uniform(splits[5], (NDATA,), jnp.float32) ** level_of(splits[5], (NDATA,), ((0, 4),), -0.2, 0.2)), 0.3, 3.0)
    depth_weight = draw_depth_weight(jax.random.fold_in(splits[8], 71), 0)
    density = bell_draw(splits[7], (NCELL,), 1.0, 6.0, ((0, 64),), jnp.float32)
    return dict(sensitivity=sensitivity, tile_rows=tile_rows, tile_cols=tile_cols, kept_counts=kept_counts, misfit=misfit, data_weight=data_weight, depth_weight=depth_weight, density=density)


damping = 1.0

def haar_matrix(tile_size):
    rows_index = jnp.arange(tile_size, dtype=jnp.int32)[:, None]
    column_index = jnp.arange(tile_size, dtype=jnp.int32)[None, :]
    levels = jnp.zeros_like(rows_index)
    for bit_shift in range(1, tile_size.bit_length()):
        levels = levels + (rows_index >= 1 << bit_shift).astype(jnp.int32)
    support = jnp.right_shift(tile_size, levels)
    offset = (rows_index - jnp.left_shift(1, levels)) * support
    inside = (column_index >= offset) & (column_index < offset + support)
    polarity = jnp.where(column_index < offset + support // 2, 1.0, -1.0)
    detail = jnp.where(inside, polarity, 0.0) / jnp.sqrt(support.astype(jnp.float32))
    coarse = jnp.full((1, tile_size), 1.0 / math.sqrt(tile_size), jnp.float32)
    return jnp.concatenate([coarse, detail[1:].astype(jnp.float32)], axis=0)

def tile_products(sensitivity, vectors, transpose):
    flattened = sensitivity.reshape(N_ROWS * N_COLS, SLOTS, TB, TB)
    stacked = vectors.reshape(N_ROWS * N_COLS, SLOTS, TB)

    def single(item):
        tile_block, vector = item
        if transpose:
            return jnp.einsum('sab,sa->sb', tile_block.astype(jnp.float32), vector.astype(jnp.float32), precision=lax.Precision.HIGHEST)
        return jnp.einsum('sab,sb->sa', tile_block.astype(jnp.float32), vector.astype(jnp.float32), precision=lax.Precision.HIGHEST)
    return lax.map(single, (flattened, stacked)).reshape(N_ROWS, N_COLS * SLOTS, TB)

def reference(sensitivity, tile_rows, tile_cols, kept_counts, misfit, data_weight, depth_weight, density):
    wavelet = haar_matrix(TB)
    live_mask = jnp.arange(TB, dtype=jnp.int32)[None, None, :] < kept_counts[:, :, None]
    group_of_slot = (jnp.arange(N_COLS * SLOTS, dtype=jnp.int32) // SLOTS).astype(jnp.int32)
    col_global = (group_of_slot[None, :] * MB + tile_cols).astype(jnp.int32)
    row_global = (jnp.arange(N_ROWS, dtype=jnp.int32)[:, None] * DB + tile_rows).astype(jnp.int32)

    def forward(cell_values):
        blocks = cell_values.reshape(N_COLS * MB, TB)
        coeffs = jnp.dot(blocks, wavelet.T, precision=lax.Precision.HIGHEST)
        picked = jnp.where(live_mask, coeffs[col_global], 0.0).astype(jnp.bfloat16)
        products = tile_products(sensitivity, picked, False)
        summed = jax.ops.segment_sum(products.reshape(-1, TB), row_global.reshape(-1), num_segments=N_ROWS * DB)
        return summed.reshape(NDATA)

    def adjoint(weighted):
        picked = weighted.reshape(N_ROWS * DB, TB)[row_global]
        products = jnp.where(live_mask, tile_products(sensitivity, picked, True), 0.0)
        block_sums = jax.ops.segment_sum(products.reshape(-1, TB), col_global.reshape(-1), num_segments=N_COLS * MB)
        return jnp.dot(block_sums, wavelet, precision=lax.Precision.HIGHEST).reshape(NCELL)
    squared = data_weight * data_weight
    rhs = depth_weight * adjoint((squared * misfit).astype(jnp.bfloat16)) - damping * density
    solution = jnp.zeros_like(density)
    residual = rhs
    direction = rhs
    change = jnp.zeros_like(misfit)
    norm_now = jnp.sum(residual * residual)
    for iteration in range(ITERS):
        image_data = forward(depth_weight * direction)
        image_cells = depth_weight * adjoint((squared * image_data).astype(jnp.bfloat16)) + damping * direction
        step_length = norm_now / jnp.sum(direction * image_cells)
        solution = solution + step_length * direction
        residual = residual - step_length * image_cells
        change = change + step_length * image_data
        norm_next = jnp.sum(residual * residual)
        direction = residual + norm_next / norm_now * direction
        norm_now = norm_next
    return (density + depth_weight * solution, misfit - change)
```

```python
import functools
import math

import jax
import jax.numpy as jnp
from jax import lax
from jax.experimental import pallas as pl
from jax.experimental.pallas import tpu as pltpu
from jax.sharding import Mesh, PartitionSpec as P

ITERS = 4
LANES = 128
SLOTS = 4
TILE = 512
CHUNKS = TILE // LANES
PRODUCT_ROWS = SLOTS * CHUNKS
MESSAGE_ROWS = PRODUCT_ROWS + 8

damping = 1.0

NN = (((1,), (0,)), ((), ()))
NT = (((1,), (1,)), ((), ()))


def haar_signs(size):
    row = lax.broadcasted_iota(jnp.int32, (size, size), 0)
    column = lax.broadcasted_iota(jnp.int32, (size, size), 1)
    level = haar_levels(row, size)
    shift = size.bit_length() - 1 - level
    place = column - jnp.left_shift(row - jnp.left_shift(1, level), shift)
    support = jnp.left_shift(1, shift)
    signs = jnp.where(place < jnp.right_shift(support, 1), 1.0, -1.0)
    signs = jnp.where((place >= 0) & (place < support), signs, 0.0)
    return jnp.where(row == 0, 1.0, signs).astype(jnp.bfloat16)


def haar_levels(row, size):
    level = jnp.zeros_like(row)
    for bit in range(1, size.bit_length() - 1):
        level = level + (row >= 1 << bit).astype(jnp.int32)
    return level


def haar_scales(size):
    row = lax.broadcasted_iota(jnp.int32, (1, size), 1)
    scales = jnp.full((1, size), 1.0 / math.sqrt(size), jnp.float32)
    for bit in range(1, size.bit_length() - 1):
        scales = jnp.where(row >= 1 << bit, math.sqrt((1 << bit) / size), scales)
    return scales


def matmul(a, b, dims):
    return lax.dot_general(a, b, dims, preferred_element_type=jnp.float32)


def split3(value):
    high = value.astype(jnp.bfloat16).astype(jnp.float32)
    rest = value - high
    middle = rest.astype(jnp.bfloat16).astype(jnp.float32)
    low = (rest - middle).astype(jnp.bfloat16).astype(jnp.float32)
    return high, middle, low


def total(values):
    return jnp.sum(jnp.sum(values, axis=0, keepdims=True), axis=1, keepdims=True)


def to_lanes(values):
    blocks = values.shape[0] // CHUNKS
    return jnp.concatenate(
        [
            jnp.concatenate(
                [values[CHUNKS * b + k : CHUNKS * b + k + 1] for k in range(CHUNKS)], axis=1
            )
            for b in range(blocks)
        ],
        axis=0,
    )


def to_rows(values):
    return jnp.concatenate(
        [
            values[b : b + 1, LANES * k : LANES * (k + 1)]
            for b in range(values.shape[0])
            for k in range(CHUNKS)
        ],
        axis=0,
    )


def times_haar(vectors, signs_ref, dims):
    parts = jnp.concatenate(split3(vectors) + (jnp.zeros((10, TILE), jnp.float32),), axis=0)
    product = matmul(parts.astype(jnp.bfloat16), signs_ref[...], dims)
    return product[0:2] + product[2:4] + product[4:6]


def slot_products(vectors, tiles_ref, dims):
    row = lax.broadcasted_iota(jnp.int32, (16, TILE), 0)
    out = jnp.zeros((16, TILE), jnp.float32)
    for s in range(SLOTS):
        out = jnp.where(row == s, matmul(vectors, tiles_ref[s], dims), out)
    return out


def adjoint(picked, masks, tiles_ref, signs_ref):
    vectors = jnp.concatenate([picked, jnp.zeros((12, TILE), jnp.float32)], axis=0)
    products = slot_products(vectors.astype(jnp.bfloat16), tiles_ref, NN)[0:SLOTS]
    sums = [
        jnp.sum(masks[SLOTS * m : SLOTS * (m + 1)] * products, axis=0, keepdims=True)
        for m in range(2)
    ]
    sums = jnp.concatenate(sums, axis=0) * haar_scales(TILE)
    return to_rows(times_haar(sums, signs_ref, NN))


def forward_message(cells, residual, direction, masks_ref, ids_ref, tiles_ref, signs_ref,
                    message_ref):
    coeffs = times_haar(to_lanes(cells), signs_ref, NT) * haar_scales(TILE)
    picked = masks_ref[0:SLOTS, :] * coeffs[0:1] + masks_ref[SLOTS : 2 * SLOTS, :] * coeffs[1:2]
    picked = jnp.concatenate([picked, jnp.zeros((12, TILE), jnp.float32)], axis=0)
    products = slot_products(picked.astype(jnp.bfloat16), tiles_ref, NT)
    norm = split3(jnp.sum(residual * residual, axis=0, keepdims=True))
    cross = split3(jnp.sum(residual * direction, axis=0, keepdims=True))
    pieces = [products[0:SLOTS, LANES * k : LANES * (k + 1)] for k in range(CHUNKS)]
    pieces += list(norm) + list(cross) + [ids_ref[0:2, :]]
    message = jnp.concatenate(pieces, axis=0).astype(jnp.bfloat16)
    message_ref[...] = jnp.broadcast_to(message[None], message_ref.shape)


def my_column():
    plane = lax.axis_index("x") * lax.axis_size("z") + lax.axis_index("z")
    return plane * lax.axis_size("core") + lax.axis_index("core")


def first_adjoint_kernel(slots_ref, weighted_ref, tiles_ref, signs_ref, part_ref, masks_ref, ids_ref,
                         pick_ref):
    rows = [slots_ref[0, s] for s in range(SLOTS)]
    column = lax.broadcasted_iota(jnp.int32, (1, TILE), 1)
    masks = jnp.concatenate(
        [
            (
                column < jnp.where(slots_ref[0, SLOTS + s] == m, slots_ref[0, 2 * SLOTS + s], 0)
            ).astype(jnp.float32)
            for m in range(2)
            for s in range(SLOTS)
        ],
        axis=0,
    )
    masks_ref[...] = masks
    picked = jnp.concatenate(
        [to_lanes(weighted_ref[pl.ds(row * CHUNKS, CHUNKS), :]) for row in rows], axis=0
    )
    part_ref[...] = adjoint(picked, masks, tiles_ref, signs_ref)
    lane = lax.broadcasted_iota(jnp.int32, (1, LANES), 1)
    row_ids = jnp.zeros((1, LANES), jnp.int32)
    for u in range(2 * SLOTS):
        row_ids = jnp.where(lane == u, rows[u % SLOTS] + (u // SLOTS) * LANES, row_ids)
    ids_ref[...] = jnp.broadcast_to(row_ids.astype(jnp.float32), ids_ref.shape)
    wide = lax.broadcasted_iota(jnp.int32, (1, 2 * LANES), 1)
    picks = [(wide == row + p * LANES).astype(jnp.float32) for p in range(2) for row in rows]
    pick_ref[...] = jnp.concatenate(
        picks + [jnp.zeros((8, 2 * LANES), jnp.float32)], axis=0
    ).astype(jnp.bfloat16)


def first_forward_kernel(masks_ref, ids_ref, tiles_ref, signs_ref, depth_ref, density_ref,
                         part0_ref, part1_ref, part2_ref, part3_ref, message_ref, residual_ref):
    sums = (part0_ref[...] + part2_ref[...]) + (part1_ref[...] + part3_ref[...])
    residual = depth_ref[...] * sums - damping * density_ref[...]
    residual_ref[...] = residual
    forward_message(depth_ref[...] * residual, residual, jnp.zeros_like(residual), masks_ref, ids_ref,
                    tiles_ref, signs_ref, message_ref)


def gathered(ref):
    values = ref[...].astype(jnp.float32)
    wide = ref.shape[0] * 8
    half = jnp.concatenate(
        [values[:, 8 * j : 8 * j + 8, :].reshape(wide, LANES) for j in range(2)], axis=1
    )
    return half.astype(jnp.bfloat16), values[:, PRODUCT_ROWS:, :]


def data_block_ids(tail):
    planes = tail.shape[0]
    wide = planes * 8
    pick = (
        lax.broadcasted_iota(jnp.int32, (16, LANES), 1)
        == lax.broadcasted_iota(jnp.int32, (16, LANES), 0)
    ).astype(jnp.bfloat16)
    spread = (
        lax.broadcasted_iota(jnp.int32, (planes, wide), 1) // 8
        == lax.broadcasted_iota(jnp.int32, (planes, wide), 0)
    ).astype(jnp.bfloat16)
    mine = lax.broadcasted_iota(jnp.int32, (16, wide), 1) % 8
    mine = mine == lax.broadcasted_iota(jnp.int32, (16, wide), 0)
    held = jnp.sum(tail[:, 6:7, :], axis=1).astype(jnp.bfloat16)
    turned = matmul(pick, held, NT).astype(jnp.bfloat16)
    return jnp.sum(jnp.where(mine, matmul(turned, spread, NN), 0.0), axis=0, keepdims=True)


def summed_field(ids, halves):
    wide = halves[0].shape[0]
    index = lax.broadcasted_iota(jnp.int32, (2 * LANES, wide), 0).astype(jnp.float32)
    return matmul((index == ids[0]).astype(jnp.bfloat16), halves[0], NN) + matmul(
        (index == ids[1]).astype(jnp.bfloat16), halves[1], NN
    )


def write_cells(cells_out_ref, direction, norm_now, direction_norm, field_ref):
    cells_out_ref[0:8, :] = direction
    cells_out_ref[8:16, :] = jnp.broadcast_to(norm_now, (8, LANES))
    cells_out_ref[16:24, :] = jnp.broadcast_to(direction_norm, (8, LANES))
    column = my_column()
    share = []
    for b in range(2):
        rows = [field_ref[pl.ds(p * LANES + 2 * column + b, 1), :] for p in range(2)]
        share += [rows[k % 2][:, LANES * (k // 2) : LANES * (k // 2 + 1)] for k in range(CHUNKS)]
    cells_out_ref[24:32, :] = jnp.concatenate(share, axis=0)


def weigh(squared, field):
    weighted = (squared * field).astype(jnp.bfloat16)
    norm = jnp.sum(
        (weighted.astype(jnp.float32) * field).reshape(2 * LANES // 8, 8, 2 * LANES), axis=0
    )
    return weighted, norm[:, :LANES] + norm[:, LANES:]


def slot_blocks(pick_ref, weighted):
    picked = matmul(pick_ref[...], weighted, NN)
    return jnp.concatenate(
        [
            picked[SLOTS * (k % 2) : SLOTS * (k % 2 + 1), LANES * (k // 2) : LANES * (k // 2 + 1)]
            for k in range(CHUNKS)
        ],
        axis=1,
    )


def first_data_kernel(masks_ref, pick_ref, tiles_ref, signs_ref, weight_ref, residual_ref,
                      own_ref, other_ref, part_ref, cells_out_ref, field_ref, ids_ref, squared_ref):
    halves, tails = zip(*(gathered(ref) for ref in (own_ref, other_ref)))
    sums = jnp.sum(tails[0] + tails[1], axis=0)
    norm_now = total(sums[0:3])
    ids = [data_block_ids(tail) for tail in tails]
    for n in range(2):
        ids_ref[n : n + 1, :] = ids[n]
    field = summed_field(ids, halves)
    field_ref[...] = field
    weight = jnp.concatenate(
        [
            jnp.concatenate(
                [weight_ref[pl.ds(2 * j + p, LANES, stride=CHUNKS), :] for j in range(2)], axis=1
            )
            for p in range(2)
        ],
        axis=0,
    )
    squared = weight * weight
    squared_ref[...] = squared
    weighted, norm_part = weigh(squared, field)
    part_ref[0:8, :] = adjoint(
        slot_blocks(pick_ref, weighted), masks_ref[...], tiles_ref, signs_ref
    )
    part_ref[8:16, :] = norm_part
    write_cells(cells_out_ref, residual_ref[...], norm_now, norm_now, field_ref)


def next_field(residual_ref, cells_ref, field_in_ref, ids_ref, own_ref, other_ref):
    halves, tails = zip(*(gathered(ref) for ref in (own_ref, other_ref)))
    sums = jnp.sum(tails[0] + tails[1], axis=0)
    norm_now = total(sums[0:3])
    cross = total(sums[3:6])
    ratio = norm_now / cells_ref[8:9, 0:1]
    field = summed_field([ids_ref[0:1, :], ids_ref[1:2, :]], halves) + ratio * field_in_ref[...]
    direction = residual_ref[0:8, :] + ratio * cells_ref[0:8, :]
    direction_norm = norm_now + ratio * (2.0 * cross + ratio * cells_ref[16:17, 0:1])
    return field, direction, norm_now, direction_norm


def data_kernel(masks_ref, pick_ref, tiles_ref, signs_ref, squared_ref, residual_ref,
                cells_ref, field_in_ref, ids_ref, own_ref, other_ref, part_ref, cells_out_ref,
                field_ref):
    field, direction, norm_now, direction_norm = next_field(
        residual_ref, cells_ref, field_in_ref, ids_ref, own_ref, other_ref
    )
    field_ref[...] = field
    weighted, norm_part = weigh(squared_ref[...], field)
    part_ref[0:8, :] = adjoint(
        slot_blocks(pick_ref, weighted), masks_ref[...], tiles_ref, signs_ref
    )
    part_ref[8:16, :] = norm_part
    write_cells(cells_out_ref, direction, norm_now, direction_norm, field_ref)


def last_data_kernel(squared_ref, residual_ref, cells_ref, field_in_ref, ids_ref, own_ref, other_ref,
                     part_ref, cells_out_ref, field_ref):
    field, direction, norm_now, direction_norm = next_field(
        residual_ref, cells_ref, field_in_ref, ids_ref, own_ref, other_ref
    )
    field_ref[...] = field
    part_ref[...] = weigh(squared_ref[...], field)[1]
    write_cells(cells_out_ref, direction, norm_now, direction_norm, field_ref)


def step_kernel(started, masks_ref, ids_ref, tiles_ref, signs_ref, depth_ref, cells_ref,
                state_ref, part0_ref, part1_ref, part2_ref, part3_ref, message_ref, state_out_ref):
    sums = (part0_ref[...] + part2_ref[...]) + (part1_ref[...] + part3_ref[...])
    direction = cells_ref[0:8, :]
    length = cells_ref[8:9, 0:1] / (total(sums[8:16]) + damping * cells_ref[16:17, 0:1])
    image = depth_ref[...] * sums[0:8] + damping * direction
    residual = state_ref[0:8, :] - length * image
    solution = length * direction
    change = length * cells_ref[24:32, :]
    if started:
        solution = state_ref[8:16, :] + solution
        change = state_ref[16:24, :] + change
    state_out_ref[0:8, :] = residual
    state_out_ref[8:16, :] = solution
    state_out_ref[16:24, :] = change
    forward_message(depth_ref[...] * residual, residual, direction, masks_ref, ids_ref, tiles_ref,
                    signs_ref, message_ref)


def last_kernel(depth_ref, density_ref, misfit_ref, cells_ref, state_ref, part0_ref, part1_ref,
                part2_ref, part3_ref, density_out_ref, misfit_out_ref):
    sums = (part0_ref[...] + part2_ref[...]) + (part1_ref[...] + part3_ref[...])
    length = cells_ref[8:9, 0:1] / (total(sums) + damping * cells_ref[16:17, 0:1])
    solution = state_ref[8:16, :] + length * cells_ref[0:8, :]
    density_out_ref[...] = density_ref[...] + depth_ref[...] * solution
    misfit_out_ref[...] = misfit_ref[...] - (state_ref[16:24, :] + length * cells_ref[24:32, :])


def shifts_along_rows(values):
    n = lax.axis_size("rows")
    opposite, left, right = (
        lax.ppermute(values, "rows", [(i, (i + step) % n) for i in range(n)]) for step in (2, 1, 3)
    )
    return values, left, opposite, right


def exchange(message):
    own = lax.all_to_all(message, ("x", "z"), 0, 0)
    return own, lax.ppermute(own, "core", [(0, 1), (1, 0)])


def call(kernel, out_shape, operands, scratch=()):
    spaces = [
        pltpu.VMEM if jnp.issubdtype(a.dtype, jnp.floating) else pltpu.SMEM for a in operands
    ]
    return pl.pallas_call(
        kernel,
        out_shape=out_shape,
        in_specs=[pl.BlockSpec(memory_space=space) for space in spaces],
        out_specs=jax.tree.map(lambda _: pl.BlockSpec(memory_space=pltpu.VMEM), out_shape),
        scratch_shapes=list(scratch),
        compiler_params=pltpu.CompilerParams(vmem_limit_bytes=24 * 2**20),
    )(*operands)


def per_device(
    sensitivity, tile_rows, tile_cols, kept_counts, misfit, data_weight, depth_weight, density
):
    tiles = sensitivity[0]
    signs = haar_signs(TILE)
    slots = jnp.concatenate([tile_rows, tile_cols, kept_counts], axis=1)
    misfit, data_weight, depth, density = (
        a.reshape(-1, LANES) for a in (misfit, data_weight, depth_weight, density)
    )
    own_misfit = lax.dynamic_slice_in_dim(misfit, my_column() * 8, 8)
    planes = lax.axis_size("x") * lax.axis_size("z")
    f32 = functools.partial(jax.ShapeDtypeStruct, dtype=jnp.float32)
    cells_shape = f32((8, LANES))
    message_shape = jax.ShapeDtypeStruct((planes, MESSAGE_ROWS, LANES), jnp.bfloat16)
    field_shape = f32((2 * LANES, 2 * LANES))
    pick_shape = jax.ShapeDtypeStruct((16, 2 * LANES), jnp.bfloat16)

    part, masks, row_ids, pick = call(
        first_adjoint_kernel,
        (cells_shape, f32((8, TILE)), cells_shape, pick_shape),
        (slots, data_weight * data_weight * misfit, tiles, signs),
    )
    forward_with = (masks, row_ids, tiles, signs)
    adjoint_with = (masks, pick, tiles, signs)
    message, state = call(
        first_forward_kernel,
        (message_shape, cells_shape),
        forward_with + (depth, density) + shifts_along_rows(part),
    )
    part, cells, field, ids, squared = call(
        first_data_kernel,
        (f32((16, LANES)), f32((32, LANES)), field_shape, f32((8, planes * 8)), field_shape),
        adjoint_with + (data_weight, state) + exchange(message),
    )
    for iteration in range(1, ITERS):
        message, state = call(
            functools.partial(step_kernel, iteration > 1),
            (message_shape, f32((24, LANES))),
            forward_with + (depth, cells, state) + shifts_along_rows(part),
        )
        carried = (squared, state, cells, field, ids) + exchange(message)
        if iteration + 1 < ITERS:
            part, cells, field = call(
                data_kernel,
                (f32((16, LANES)), f32((32, LANES)), field_shape),
                adjoint_with + carried,
            )
    part, cells = call(
        last_data_kernel,
        (cells_shape, f32((32, LANES))),
        carried,
        [pltpu.VMEM(field_shape.shape, jnp.float32)],
    )
    new_density, new_misfit = call(
        last_kernel,
        (cells_shape, cells_shape),
        (depth, density, own_misfit, cells, state) + shifts_along_rows(part),
    )
    return (new_density.reshape(-1), new_misfit.reshape(-1))


def solution(mesh):
    cols = ("x", "z", "core")
    fine = Mesh(mesh.devices.reshape(4, 4, 8, 2), ("rows",) + cols)
    return jax.shard_map(
        per_device,
        mesh=fine,
        in_specs=(
            P("rows", cols, None, None),
            P("rows", cols),
            P("rows", cols),
            P("rows", cols),
            P("rows"),
            P("rows"),
            P(cols),
            P(cols),
        ),
        out_specs=(P(cols), P(("rows",) + cols)),
        check_vma=False,
    )
```

```python
import functools
import math

import jax
import jax.numpy as jnp
from jax import lax
from jax.experimental import pallas as pl
from jax.experimental.pallas import tpu as pltpu
from jax.sharding import Mesh, PartitionSpec as P

ITERS = 4
LANES = 128
SLOTS = 4
TILE = 512
CHUNKS = TILE // LANES
PRODUCT_ROWS = SLOTS * CHUNKS
MESSAGE_ROWS = PRODUCT_ROWS + 8
FINE = (0, 1, 2, 3)

damping = 1.0

NN = (((1,), (0,)), ((), ()))
NT = (((1,), (1,)), ((), ()))


def haar_signs(size):
    row = lax.broadcasted_iota(jnp.int32, (size, size), 0)
    column = lax.broadcasted_iota(jnp.int32, (size, size), 1)
    level = haar_levels(row, size)
    shift = size.bit_length() - 1 - level
    place = column - jnp.left_shift(row - jnp.left_shift(1, level), shift)
    support = jnp.left_shift(1, shift)
    signs = jnp.where(place < jnp.right_shift(support, 1), 1.0, -1.0)
    signs = jnp.where((place >= 0) & (place < support), signs, 0.0)
    return jnp.where(row == 0, 1.0, signs).astype(jnp.bfloat16)


def haar_levels(row, size):
    level = jnp.zeros_like(row)
    for bit in range(1, size.bit_length() - 1):
        level = level + (row >= 1 << bit).astype(jnp.int32)
    return level


def haar_scales(size):
    row = lax.broadcasted_iota(jnp.int32, (1, size), 1)
    scales = jnp.full((1, size), 1.0 / math.sqrt(size), jnp.float32)
    for bit in range(1, size.bit_length() - 1):
        scales = jnp.where(row >= 1 << bit, math.sqrt((1 << bit) / size), scales)
    return scales


def matmul(a, b, dims):
    return lax.dot_general(a, b, dims, preferred_element_type=jnp.float32)


def split3(value):
    high = value.astype(jnp.bfloat16).astype(jnp.float32)
    rest = value - high
    middle = rest.astype(jnp.bfloat16).astype(jnp.float32)
    low = (rest - middle).astype(jnp.bfloat16).astype(jnp.float32)
    return high, middle, low


def total(values):
    return jnp.sum(jnp.sum(values, axis=0, keepdims=True), axis=1, keepdims=True)


def to_rows(values):
    return jnp.concatenate(
        [
            values[b : b + 1, LANES * k : LANES * (k + 1)]
            for b in range(values.shape[0])
            for k in range(CHUNKS)
        ],
        axis=0,
    )


def lane_parts(values):
    parts = sum(values[:, LANES * k : LANES * (k + 1)] for k in range(1, CHUNKS))
    return jnp.sum(values[:, :LANES] + parts, axis=0, keepdims=True)


def times_haar(vectors, signs_ref, dims):
    parts = jnp.concatenate(split3(vectors) + (jnp.zeros((10, TILE), jnp.float32),), axis=0)
    product = matmul(parts.astype(jnp.bfloat16), signs_ref[...], dims)
    return product[0:2] + product[2:4] + product[4:6]


def slot_products(vectors, tiles_ref, dims):
    vectors = jnp.concatenate([vectors, jnp.zeros((12, TILE), jnp.float32)], axis=0)
    vectors = vectors.astype(jnp.bfloat16)
    row = lax.broadcasted_iota(jnp.int32, (SLOTS, TILE), 0)
    out = jnp.zeros((SLOTS, TILE), jnp.float32)
    for s in range(SLOTS):
        out = jnp.where(row == s, matmul(vectors, tiles_ref[s], dims)[0:SLOTS], out)
    return out


def adjoint_sums(picked, masks_ref, tiles_ref):
    products = slot_products(picked, tiles_ref, NN)
    sums = [
        jnp.sum(masks_ref[SLOTS * m : SLOTS * (m + 1), :] * products, axis=0, keepdims=True)
        for m in range(2)
    ]
    return jnp.concatenate(sums, axis=0)


def summed_cells(sums, signs_ref):
    return times_haar(sums * haar_scales(TILE), signs_ref, NN)


def forward_message(cells, residual, direction, masks_ref, ids_ref, tiles_ref, analysis_ref,
                    message_ref, dims):
    coeffs = times_haar(cells, analysis_ref, dims) * haar_scales(TILE)
    picked = masks_ref[0:SLOTS, :] * coeffs[0:1] + masks_ref[SLOTS : 2 * SLOTS, :] * coeffs[1:2]
    products = slot_products(picked, tiles_ref, dims)
    norm = split3(lane_parts(residual * residual))
    cross = split3(lane_parts(residual * direction))
    high, low, _ = split3(products)
    sent = (high, low) if message_ref.shape[1] > MESSAGE_ROWS else (high,)
    pieces = [part[:, LANES * k : LANES * (k + 1)] for part in sent for k in range(CHUNKS)]
    pieces += list(norm) + list(cross) + [ids_ref[0:2, :]]
    message = jnp.concatenate(pieces, axis=0).astype(jnp.bfloat16)
    message_ref[...] = jnp.broadcast_to(message[None], message_ref.shape)


def my_plane():
    return lax.axis_index("x") * lax.axis_size("z") + lax.axis_index("z")


def my_column():
    return my_plane() * lax.axis_size("core") + lax.axis_index("core")


def turn_kernel(tiles_ref, signs_ref, turned_ref, analysis_ref):
    for s in range(SLOTS):
        turned_ref[s] = tiles_ref[s].T
    analysis_ref[...] = signs_ref[...].T


def prepare_kernel(slots_ref, weight_ref, masks_ref, ids_ref, pick_ref, squared_ref):
    rows = [slots_ref[0, s] for s in range(SLOTS)]
    column = lax.broadcasted_iota(jnp.int32, (1, TILE), 1)
    masks_ref[...] = jnp.concatenate(
        [
            (
                column < jnp.where(slots_ref[0, SLOTS + s] == m, slots_ref[0, 2 * SLOTS + s], 0)
            ).astype(jnp.float32)
            for m in range(2)
            for s in range(SLOTS)
        ],
        axis=0,
    )
    lane = lax.broadcasted_iota(jnp.int32, (8, LANES), 1)
    plane = lax.broadcasted_iota(jnp.int32, (8, LANES), 0) * (LANES // 8) + lane // 8
    row_ids = jnp.zeros((8, LANES), jnp.int32)
    for u in range(2 * SLOTS):
        row_ids = jnp.where(lane % 8 == u, rows[u % SLOTS] + (u // SLOTS) * LANES, row_ids)
    ids_ref[...] = jnp.where(plane == my_plane(), row_ids, 0).astype(jnp.float32)
    wide = lax.broadcasted_iota(jnp.int32, (1, 2 * LANES), 1)
    picks = [(wide == row + p * LANES).astype(jnp.float32) for p in range(2) for row in rows]
    pick_ref[...] = jnp.concatenate(
        picks + [jnp.zeros((8, 2 * LANES), jnp.float32)], axis=0
    ).astype(jnp.bfloat16)
    for p in range(2):
        for j in range(2):
            weight = weight_ref[pl.ds(2 * j + p, LANES, stride=CHUNKS), :]
            squared_ref[LANES * p : LANES * (p + 1), LANES * j : LANES * (j + 1)] = weight * weight


def first_forward_kernel(masks_ref, ids_ref, tiles_ref, signs_ref, depth_ref, density_ref, part0_ref,
                         part1_ref, part2_ref, part3_ref, message_ref, residual_ref):
    sums = (part0_ref[...] + part2_ref[...]) + (part1_ref[...] + part3_ref[...])
    residual = depth_ref[...] * summed_cells(sums, signs_ref) - damping * density_ref[...]
    residual_ref[...] = residual
    forward_message(depth_ref[...] * residual, residual, jnp.zeros_like(residual), masks_ref, ids_ref,
                    tiles_ref, signs_ref, message_ref, NT)


def gathered(ref):
    values = ref[...].astype(jnp.float32)
    wide = ref.shape[0] * 8
    last = ref.shape[1] - 8
    halves = [
        jnp.concatenate(
            [values[:, n + 8 * j : n + 8 * j + 8, :].reshape(wide, LANES) for j in range(2)], axis=1
        ).astype(jnp.bfloat16)
        for n in range(0, last, PRODUCT_ROWS)
    ]
    return halves, jnp.sum(values[:, last:, :], axis=0)


def summed_field(ids, halves):
    wide = halves[0][0].shape[0]
    index = lax.broadcasted_iota(jnp.int32, (2 * LANES, wide), 0).astype(jnp.float32)
    fields = []
    for row, parts in zip(ids, halves):
        place = (index == row).astype(jnp.bfloat16)
        fields.append(sum(matmul(place, part, NN) for part in parts[::-1]))
    return fields[0] + fields[1]


def write_scalars(scalars_ref, share_ref, norm_now, direction_norm, field_ref):
    scalars_ref[0:8, :] = jnp.broadcast_to(norm_now, (8, LANES))
    scalars_ref[8:16, :] = jnp.broadcast_to(direction_norm, (8, LANES))
    column = my_column()
    share = []
    for b in range(2):
        rows = [field_ref[pl.ds(p * LANES + 2 * column + b, 1), :] for p in range(2)]
        share += [rows[k % 2][:, LANES * (k // 2) : LANES * (k // 2 + 1)] for k in range(CHUNKS)]
    share_ref[...] = jnp.concatenate(share, axis=0)


def weigh(squared, field):
    weighted = (squared * field).astype(jnp.bfloat16)
    norm = jnp.sum(
        (weighted.astype(jnp.float32) * field).reshape(2 * LANES // 8, 8, 2 * LANES), axis=0
    )
    norm = norm[:, :LANES] + norm[:, LANES:]
    return weighted, (norm[0:2] + norm[2:4]) + (norm[4:6] + norm[6:8])


def slot_blocks(pick_ref, weighted):
    picked = matmul(pick_ref[...], weighted, NN)
    return jnp.concatenate(
        [
            picked[SLOTS * (k % 2) : SLOTS * (k % 2 + 1), LANES * (k // 2) : LANES * (k // 2 + 1)]
            for k in range(CHUNKS)
        ],
        axis=1,
    )


def write_parts(part_ref, norm_part, weighted, masks_ref, pick_ref, tiles_ref):
    part_ref[:, 0:TILE] = adjoint_sums(slot_blocks(pick_ref, weighted), masks_ref, tiles_ref)
    part_ref[:, TILE:] = norm_part


def first_data_kernel(masks_ref, pick_ref, tiles_ref, squared_ref, own_ref, other_ref, part_ref,
                      scalars_ref, share_ref, field_ref, ids_ref):
    halves, tails = zip(*(gathered(ref) for ref in (own_ref, other_ref)))
    norm_now = total((tails[0] + tails[1])[0:3])
    ids = [jnp.concatenate([tail[6:7], tail[7:8]], axis=1) for tail in tails]
    for n in range(2):
        ids_ref[n : n + 1, :] = ids[n]
    field = summed_field(ids, halves)
    field_ref[...] = field
    weighted, norm_part = weigh(squared_ref[...], field)
    write_parts(part_ref, norm_part, weighted, masks_ref, pick_ref, tiles_ref)
    write_scalars(scalars_ref, share_ref, norm_now, norm_now, field_ref)


def next_field(residual_ref, direction_in_ref, scalars_in_ref, field_in_ref, ids_ref, own_ref, other_ref):
    halves, tails = zip(*(gathered(ref) for ref in (own_ref, other_ref)))
    sums = tails[0] + tails[1]
    norm_now = total(sums[0:3])
    cross = total(sums[3:6])
    ratio = norm_now / scalars_in_ref[0:1, 0:1]
    field = summed_field([ids_ref[0:1, :], ids_ref[1:2, :]], halves) + ratio * field_in_ref[...]
    direction = residual_ref[...] + ratio * direction_in_ref[...]
    direction_norm = norm_now + ratio * (2.0 * cross + ratio * scalars_in_ref[8:9, 0:1])
    return field, direction, norm_now, direction_norm


def data_kernel(masks_ref, pick_ref, tiles_ref, squared_ref, residual_ref, direction_in_ref,
                scalars_in_ref, field_in_ref, ids_ref, own_ref, other_ref, part_ref, direction_ref,
                scalars_ref, share_ref, field_ref):
    field, direction, norm_now, direction_norm = next_field(
        residual_ref, direction_in_ref, scalars_in_ref, field_in_ref, ids_ref, own_ref, other_ref
    )
    field_ref[...] = field
    direction_ref[...] = direction
    weighted, norm_part = weigh(squared_ref[...], field)
    write_parts(part_ref, norm_part, weighted, masks_ref, pick_ref, tiles_ref)
    write_scalars(scalars_ref, share_ref, norm_now, direction_norm, field_ref)


def last_data_kernel(squared_ref, residual_ref, direction_in_ref, scalars_in_ref, field_in_ref, ids_ref,
                     own_ref, other_ref, part_ref, direction_ref, scalars_ref, share_ref, field_ref):
    field, direction, norm_now, direction_norm = next_field(
        residual_ref, direction_in_ref, scalars_in_ref, field_in_ref, ids_ref, own_ref, other_ref
    )
    field_ref[...] = field
    direction_ref[...] = direction
    part_ref[...] = weigh(squared_ref[...], field)[1]
    write_scalars(scalars_ref, share_ref, norm_now, direction_norm, field_ref)


def step_kernel(started, *refs):
    masks_ref, ids_ref, tiles_ref, signs_ref, analysis_ref, depth_ref = refs[:6]
    residual_in_ref, direction_ref, scalars_ref, share_ref = refs[6:10]
    refs = refs[10:]
    if started:
        solution_in_ref, change_in_ref = refs[:2]
        refs = refs[2:]
    part0_ref, part1_ref, part2_ref, part3_ref = refs[:4]
    message_ref, residual_ref, solution_ref, change_ref = refs[4:]
    sums = (part0_ref[...] + part2_ref[...]) + (part1_ref[...] + part3_ref[...])
    direction = direction_ref[...]
    length = scalars_ref[0:1, 0:1] / (total(sums[:, TILE:]) + damping * scalars_ref[8:9, 0:1])
    image = depth_ref[...] * summed_cells(sums[:, 0:TILE], signs_ref) + damping * direction
    residual = residual_in_ref[...] - length * image
    residual_ref[...] = residual
    solution = length * direction
    change = length * share_ref[...]
    if started:
        solution = solution_in_ref[...] + solution
        change = change_in_ref[...] + change
    solution_ref[...] = solution
    change_ref[...] = change
    forward_message(depth_ref[...] * residual, residual, direction, masks_ref, ids_ref, tiles_ref,
                    analysis_ref, message_ref, NN)


def last_kernel(depth_ref, density_ref, misfit_ref, direction_ref, scalars_ref, share_ref, solution_ref,
                change_ref, part0_ref, part1_ref, part2_ref, part3_ref, density_out_ref,
                misfit_out_ref):
    sums = (part0_ref[...] + part2_ref[...]) + (part1_ref[...] + part3_ref[...])
    length = scalars_ref[0:1, 0:1] / (total(sums) + damping * scalars_ref[8:9, 0:1])
    solution = solution_ref[...] + length * direction_ref[...]
    density_out_ref[...] = to_rows(density_ref[...] + depth_ref[...] * solution)
    misfit_out_ref[...] = misfit_ref[...] - (change_ref[...] + length * share_ref[...])


def shifts_along_rows(values):
    n = lax.axis_size("rows")
    opposite, left, right = (
        lax.ppermute(values, "rows", [(i, (i + step) % n) for i in range(n)]) for step in (2, 1, 3)
    )
    return values, left, opposite, right


def exchange(message):
    own = lax.all_to_all(message, ("x", "z"), 0, 0)
    return own, lax.ppermute(own, "core", [(0, 1), (1, 0)])


def call(kernel, out_shape, operands, scratch=()):
    spaces = [
        pltpu.VMEM if jnp.issubdtype(a.dtype, jnp.floating) else pltpu.SMEM for a in operands
    ]
    return pl.pallas_call(
        kernel,
        out_shape=out_shape,
        in_specs=[pl.BlockSpec(memory_space=space) for space in spaces],
        out_specs=jax.tree.map(lambda _: pl.BlockSpec(memory_space=pltpu.VMEM), out_shape),
        scratch_shapes=list(scratch),
        compiler_params=pltpu.CompilerParams(vmem_limit_bytes=24 * 2**20),
    )(*operands)


def first_sums(tiles, slot_rows, slot_cols, slot_kept, misfit, data_weight):
    weighted = (data_weight * data_weight * misfit).astype(jnp.bfloat16).reshape(-1, TILE)
    blocks = jnp.arange(weighted.shape[0], dtype=jnp.int32)
    picked = jnp.dot(
        (slot_rows[:, None] == blocks[None, :]).astype(jnp.bfloat16),
        weighted,
        preferred_element_type=jnp.float32,
    ).astype(jnp.bfloat16)
    products = jnp.einsum("sab,sa->sb", tiles, picked, preferred_element_type=jnp.float32)
    live = jnp.arange(TILE, dtype=jnp.int32)[None, :] < slot_kept[:, None]
    products = jnp.where(live, products, 0.0)
    pick_cols = slot_cols[None, :] == jnp.arange(2, dtype=jnp.int32)[:, None]
    return jnp.dot(pick_cols.astype(jnp.float32), products, precision=lax.Precision.HIGHEST)


def per_device(
    sensitivity, tile_rows, tile_cols, kept_counts, misfit, data_weight, depth_weight, density
):
    tiles = sensitivity[0]
    signs = haar_signs(TILE)
    turned, analysis = call(
        turn_kernel,
        tuple(jax.ShapeDtypeStruct(a.shape, a.dtype) for a in (tiles, signs)),
        (tiles, signs),
    )
    slots = jnp.concatenate([tile_rows, tile_cols, kept_counts], axis=1)
    depth, density = (a.reshape(2, TILE) for a in (depth_weight, density))
    own_misfit = lax.dynamic_slice_in_dim(misfit.reshape(-1, LANES), my_column() * 8, 8)
    planes = lax.axis_size("x") * lax.axis_size("z")
    f32 = functools.partial(jax.ShapeDtypeStruct, dtype=jnp.float32)
    cells, rows, parts = f32((2, TILE)), f32((8, LANES)), f32((2, TILE + LANES))
    scalars_shape, field_shape = f32((16, LANES)), f32((2 * LANES, 2 * LANES))
    message_shapes = [
        jax.ShapeDtypeStruct(
            (planes, MESSAGE_ROWS + (PRODUCT_ROWS if n in FINE else 0), LANES), jnp.bfloat16
        )
        for n in range(ITERS)
    ]
    pick_shape = jax.ShapeDtypeStruct((16, 2 * LANES), jnp.bfloat16)

    masks, row_ids, pick, squared = call(
        prepare_kernel,
        (f32((8, TILE)), rows, pick_shape, field_shape),
        (slots, data_weight.reshape(-1, LANES)),
    )
    part = first_sums(tiles, tile_rows[0], tile_cols[0], kept_counts[0], misfit, data_weight)
    message, residual = call(
        first_forward_kernel,
        (message_shapes[0], cells),
        (masks, row_ids, tiles, signs, depth, density) + shifts_along_rows(part),
    )
    part, scalars, share, field, ids = call(
        first_data_kernel,
        (parts, scalars_shape, rows, field_shape, f32((8, planes * 8))),
        (masks, pick, tiles, squared) + exchange(message),
    )
    direction = residual
    sofar = ()
    for iteration in range(1, ITERS):
        message, residual, *sofar = call(
            functools.partial(step_kernel, iteration > 1),
            (message_shapes[iteration], cells, cells, rows),
            (masks, row_ids, turned, signs, analysis, depth, residual, direction, scalars, share)
            + (*sofar, *shifts_along_rows(part)),
        )
        carried = (squared, residual, direction, scalars, field, ids) + exchange(message)
        if iteration + 1 < ITERS:
            part, direction, scalars, share, field = call(
                data_kernel,
                (parts, cells, scalars_shape, rows, field_shape),
                (masks, pick, tiles) + carried,
            )
    part, direction, scalars, share = call(
        last_data_kernel,
        (f32((2, LANES)), cells, scalars_shape, rows),
        carried,
        [pltpu.VMEM(field_shape.shape, jnp.float32)],
    )
    new_density, new_misfit = call(
        last_kernel,
        (rows, rows),
        (depth, density, own_misfit, direction, scalars, share, *sofar) + shifts_along_rows(part),
    )
    return (new_density.reshape(-1), new_misfit.reshape(-1))


def solution(mesh):
    cols = ("x", "z", "core")
    fine = Mesh(mesh.devices.reshape(4, 4, 8, 2), ("rows",) + cols)
    return jax.shard_map(
        per_device,
        mesh=fine,
        in_specs=(
            P("rows", cols, None, None),
            P("rows", cols),
            P("rows", cols),
            P("rows", cols),
            P("rows"),
            P("rows"),
            P(cols),
            P(cols),
        ),
        out_specs=(P(cols), P(("rows",) + cols)),
        check_vma=False,
    )
```

```python
import functools
import math

import jax
import jax.numpy as jnp
from jax import lax
from jax.experimental import pallas as pl
from jax.experimental.pallas import tpu as pltpu
from jax.sharding import Mesh, PartitionSpec as P

ITERS = 4
LANES = 128
SLOTS = 4
TILE = 512
CHUNKS = TILE // LANES
PRODUCT_ROWS = SLOTS * CHUNKS
MESSAGE_ROWS = PRODUCT_ROWS + 8
FINE = (0, 1)

damping = 1.0

NN = (((1,), (0,)), ((), ()))
NT = (((1,), (1,)), ((), ()))


def haar_signs(size):
    row = lax.broadcasted_iota(jnp.int32, (size, size), 0)
    column = lax.broadcasted_iota(jnp.int32, (size, size), 1)
    level = haar_levels(row, size)
    shift = size.bit_length() - 1 - level
    place = column - jnp.left_shift(row - jnp.left_shift(1, level), shift)
    support = jnp.left_shift(1, shift)
    signs = jnp.where(place < jnp.right_shift(support, 1), 1.0, -1.0)
    signs = jnp.where((place >= 0) & (place < support), signs, 0.0)
    return jnp.where(row == 0, 1.0, signs).astype(jnp.bfloat16)


def haar_levels(row, size):
    level = jnp.zeros_like(row)
    for bit in range(1, size.bit_length() - 1):
        level = level + (row >= 1 << bit).astype(jnp.int32)
    return level


def haar_scales(size):
    row = lax.broadcasted_iota(jnp.int32, (1, size), 1)
    scales = jnp.full((1, size), 1.0 / math.sqrt(size), jnp.float32)
    for bit in range(1, size.bit_length() - 1):
        scales = jnp.where(row >= 1 << bit, math.sqrt((1 << bit) / size), scales)
    return scales


def matmul(a, b, dims):
    return lax.dot_general(a, b, dims, preferred_element_type=jnp.float32)


def split3(value):
    high = value.astype(jnp.bfloat16).astype(jnp.float32)
    rest = value - high
    middle = rest.astype(jnp.bfloat16).astype(jnp.float32)
    low = (rest - middle).astype(jnp.bfloat16).astype(jnp.float32)
    return high, middle, low


def total(values):
    return jnp.sum(jnp.sum(values, axis=0, keepdims=True), axis=1, keepdims=True)


def to_rows(values):
    return jnp.concatenate(
        [
            values[b : b + 1, LANES * k : LANES * (k + 1)]
            for b in range(values.shape[0])
            for k in range(CHUNKS)
        ],
        axis=0,
    )


def lane_parts(values):
    parts = sum(values[:, LANES * k : LANES * (k + 1)] for k in range(1, CHUNKS))
    return jnp.sum(values[:, :LANES] + parts, axis=0, keepdims=True)


def times_haar(vectors, signs_ref, dims):
    parts = jnp.concatenate(split3(vectors) + (jnp.zeros((10, TILE), jnp.float32),), axis=0)
    product = matmul(parts.astype(jnp.bfloat16), signs_ref[...], dims)
    return product[0:2] + product[2:4] + product[4:6]


def slot_products(vectors, tiles_ref, dims):
    vectors = jnp.concatenate([vectors, jnp.zeros((12, TILE), jnp.float32)], axis=0)
    vectors = vectors.astype(jnp.bfloat16)
    row = lax.broadcasted_iota(jnp.int32, (SLOTS, TILE), 0)
    out = jnp.zeros((SLOTS, TILE), jnp.float32)
    for s in range(SLOTS):
        out = jnp.where(row == s, matmul(vectors, tiles_ref[s], dims)[0:SLOTS], out)
    return out


def adjoint_sums(picked, masks_ref, tiles_ref):
    products = slot_products(picked, tiles_ref, NN)
    sums = [
        jnp.sum(masks_ref[SLOTS * m : SLOTS * (m + 1), :] * products, axis=0, keepdims=True)
        for m in range(2)
    ]
    return jnp.concatenate(sums, axis=0)


def summed_cells(sums, signs_ref):
    return times_haar(sums * haar_scales(TILE), signs_ref, NN)


def forward_message(cells, residual, direction, masks_ref, ids_ref, tiles_ref, analysis_ref,
                    message_ref, dims):
    coeffs = times_haar(cells, analysis_ref, dims) * haar_scales(TILE)
    picked = masks_ref[0:SLOTS, :] * coeffs[0:1] + masks_ref[SLOTS : 2 * SLOTS, :] * coeffs[1:2]
    products = slot_products(picked, tiles_ref, dims)
    norm = split3(lane_parts(residual * residual))
    cross = split3(lane_parts(residual * direction))
    high, low, _ = split3(products)
    sent = (high, low) if message_ref.shape[1] > MESSAGE_ROWS else (high,)
    pieces = [part[:, LANES * k : LANES * (k + 1)] for part in sent for k in range(CHUNKS)]
    pieces += list(norm) + list(cross) + [ids_ref[0:2, :]]
    message = jnp.concatenate(pieces, axis=0).astype(jnp.bfloat16)
    message_ref[...] = jnp.broadcast_to(message[None], message_ref.shape)


def my_plane():
    return lax.axis_index("x") * lax.axis_size("z") + lax.axis_index("z")


def my_column():
    return my_plane() * lax.axis_size("core") + lax.axis_index("core")


def turn_kernel(tiles_ref, signs_ref, turned_ref, analysis_ref):
    for s in range(SLOTS):
        turned_ref[s] = tiles_ref[s].T
    analysis_ref[...] = signs_ref[...].T


def prepare_kernel(slots_ref, weight_ref, masks_ref, ids_ref, pick_ref, squared_ref):
    rows = [slots_ref[0, s] for s in range(SLOTS)]
    column = lax.broadcasted_iota(jnp.int32, (1, TILE), 1)
    masks_ref[...] = jnp.concatenate(
        [
            (
                column < jnp.where(slots_ref[0, SLOTS + s] == m, slots_ref[0, 2 * SLOTS + s], 0)
            ).astype(jnp.float32)
            for m in range(2)
            for s in range(SLOTS)
        ],
        axis=0,
    )
    lane = lax.broadcasted_iota(jnp.int32, (8, LANES), 1)
    plane = lax.broadcasted_iota(jnp.int32, (8, LANES), 0) * (LANES // 8) + lane // 8
    row_ids = jnp.zeros((8, LANES), jnp.int32)
    for u in range(2 * SLOTS):
        row_ids = jnp.where(lane % 8 == u, rows[u % SLOTS] + (u // SLOTS) * LANES, row_ids)
    ids_ref[...] = jnp.where(plane == my_plane(), row_ids, 0).astype(jnp.float32)
    wide = lax.broadcasted_iota(jnp.int32, (1, 2 * LANES), 1)
    picks = [(wide == row + p * LANES).astype(jnp.float32) for p in range(2) for row in rows]
    pick_ref[...] = jnp.concatenate(
        picks + [jnp.zeros((8, 2 * LANES), jnp.float32)], axis=0
    ).astype(jnp.bfloat16)
    for p in range(2):
        for j in range(2):
            weight = weight_ref[pl.ds(2 * j + p, LANES, stride=CHUNKS), :]
            squared_ref[LANES * p : LANES * (p + 1), LANES * j : LANES * (j + 1)] = weight * weight


def first_forward_kernel(masks_ref, ids_ref, tiles_ref, signs_ref, depth_ref, density_ref, part0_ref,
                         part1_ref, part2_ref, part3_ref, message_ref, residual_ref):
    sums = (part0_ref[...] + part2_ref[...]) + (part1_ref[...] + part3_ref[...])
    residual = depth_ref[...] * summed_cells(sums, signs_ref) - damping * density_ref[...]
    residual_ref[...] = residual
    forward_message(depth_ref[...] * residual, residual, jnp.zeros_like(residual), masks_ref, ids_ref,
                    tiles_ref, signs_ref, message_ref, NT)


def gathered(ref):
    values = ref[...].astype(jnp.float32)
    wide = ref.shape[0] * 8
    last = ref.shape[1] - 8
    halves = [
        jnp.concatenate(
            [values[:, n + 8 * j : n + 8 * j + 8, :].reshape(wide, LANES) for j in range(2)], axis=1
        ).astype(jnp.bfloat16)
        for n in range(0, last, PRODUCT_ROWS)
    ]
    return halves, jnp.sum(values[:, last:, :], axis=0)


def summed_field(ids, halves):
    wide = halves[0][0].shape[0]
    index = lax.broadcasted_iota(jnp.int32, (2 * LANES, wide), 0).astype(jnp.float32)
    fields = []
    for row, parts in zip(ids, halves):
        place = (index == row).astype(jnp.bfloat16)
        fields.append(sum(matmul(place, part, NN) for part in parts[::-1]))
    return fields[0] + fields[1]


def write_scalars(scalars_ref, share_ref, norm_now, direction_norm, field_ref):
    scalars_ref[0:8, :] = jnp.broadcast_to(norm_now, (8, LANES))
    scalars_ref[8:16, :] = jnp.broadcast_to(direction_norm, (8, LANES))
    column = my_column()
    share = []
    for b in range(2):
        rows = [field_ref[pl.ds(p * LANES + 2 * column + b, 1), :] for p in range(2)]
        share += [rows[k % 2][:, LANES * (k // 2) : LANES * (k // 2 + 1)] for k in range(CHUNKS)]
    share_ref[...] = jnp.concatenate(share, axis=0)


def weigh(squared, field):
    weighted = (squared * field).astype(jnp.bfloat16)
    norm = jnp.sum(
        (weighted.astype(jnp.float32) * field).reshape(2 * LANES // 8, 8, 2 * LANES), axis=0
    )
    norm = norm[:, :LANES] + norm[:, LANES:]
    return weighted, (norm[0:2] + norm[2:4]) + (norm[4:6] + norm[6:8])


def slot_blocks(pick_ref, weighted):
    picked = matmul(pick_ref[...], weighted, NN)
    return jnp.concatenate(
        [
            picked[SLOTS * (k % 2) : SLOTS * (k % 2 + 1), LANES * (k // 2) : LANES * (k // 2 + 1)]
            for k in range(CHUNKS)
        ],
        axis=1,
    )


def write_parts(part_ref, norm_part, weighted, masks_ref, pick_ref, tiles_ref):
    part_ref[:, 0:TILE] = adjoint_sums(slot_blocks(pick_ref, weighted), masks_ref, tiles_ref)
    part_ref[:, TILE:] = norm_part


def first_data_kernel(masks_ref, pick_ref, tiles_ref, squared_ref, own_ref, other_ref, part_ref,
                      scalars_ref, share_ref, field_ref, ids_ref):
    halves, tails = zip(*(gathered(ref) for ref in (own_ref, other_ref)))
    norm_now = total((tails[0] + tails[1])[0:3])
    ids = [jnp.concatenate([tail[6:7], tail[7:8]], axis=1) for tail in tails]
    for n in range(2):
        ids_ref[n : n + 1, :] = ids[n]
    field = summed_field(ids, halves)
    field_ref[...] = field
    weighted, norm_part = weigh(squared_ref[...], field)
    write_parts(part_ref, norm_part, weighted, masks_ref, pick_ref, tiles_ref)
    write_scalars(scalars_ref, share_ref, norm_now, norm_now, field_ref)


def next_field(residual_ref, direction_in_ref, scalars_in_ref, field_in_ref, ids_ref, own_ref, other_ref):
    halves, tails = zip(*(gathered(ref) for ref in (own_ref, other_ref)))
    sums = tails[0] + tails[1]
    norm_now = total(sums[0:3])
    cross = total(sums[3:6])
    ratio = norm_now / scalars_in_ref[0:1, 0:1]
    field = summed_field([ids_ref[0:1, :], ids_ref[1:2, :]], halves) + ratio * field_in_ref[...]
    direction = residual_ref[...] + ratio * direction_in_ref[...]
    direction_norm = norm_now + ratio * (2.0 * cross + ratio * scalars_in_ref[8:9, 0:1])
    return field, direction, norm_now, direction_norm


def data_kernel(masks_ref, pick_ref, tiles_ref, squared_ref, residual_ref, direction_in_ref,
                scalars_in_ref, field_in_ref, ids_ref, own_ref, other_ref, part_ref, direction_ref,
                scalars_ref, share_ref, field_ref):
    field, direction, norm_now, direction_norm = next_field(
        residual_ref, direction_in_ref, scalars_in_ref, field_in_ref, ids_ref, own_ref, other_ref
    )
    field_ref[...] = field
    direction_ref[...] = direction
    weighted, norm_part = weigh(squared_ref[...], field)
    write_parts(part_ref, norm_part, weighted, masks_ref, pick_ref, tiles_ref)
    write_scalars(scalars_ref, share_ref, norm_now, direction_norm, field_ref)


def last_data_kernel(squared_ref, residual_ref, direction_in_ref, scalars_in_ref, field_in_ref, ids_ref,
                     own_ref, other_ref, part_ref, direction_ref, scalars_ref, share_ref, field_ref):
    field, direction, norm_now, direction_norm = next_field(
        residual_ref, direction_in_ref, scalars_in_ref, field_in_ref, ids_ref, own_ref, other_ref
    )
    field_ref[...] = field
    direction_ref[...] = direction
    part_ref[...] = weigh(squared_ref[...], field)[1]
    write_scalars(scalars_ref, share_ref, norm_now, direction_norm, field_ref)


def step_kernel(started, *refs):
    masks_ref, ids_ref, tiles_ref, signs_ref, analysis_ref, depth_ref = refs[:6]
    residual_in_ref, direction_ref, scalars_ref, share_ref = refs[6:10]
    refs = refs[10:]
    if started:
        solution_in_ref, change_in_ref = refs[:2]
        refs = refs[2:]
    part0_ref, part1_ref, part2_ref, part3_ref = refs[:4]
    message_ref, residual_ref, solution_ref, change_ref = refs[4:]
    sums = (part0_ref[...] + part2_ref[...]) + (part1_ref[...] + part3_ref[...])
    direction = direction_ref[...]
    length = scalars_ref[0:1, 0:1] / (total(sums[:, TILE:]) + damping * scalars_ref[8:9, 0:1])
    image = depth_ref[...] * summed_cells(sums[:, 0:TILE], signs_ref) + damping * direction
    residual = residual_in_ref[...] - length * image
    residual_ref[...] = residual
    solution = length * direction
    change = length * share_ref[...]
    if started:
        solution = solution_in_ref[...] + solution
        change = change_in_ref[...] + change
    solution_ref[...] = solution
    change_ref[...] = change
    forward_message(depth_ref[...] * residual, residual, direction, masks_ref, ids_ref, tiles_ref,
                    analysis_ref, message_ref, NN)


def last_kernel(depth_ref, density_ref, misfit_ref, direction_ref, scalars_ref, share_ref, solution_ref,
                change_ref, part0_ref, part1_ref, part2_ref, part3_ref, density_out_ref,
                misfit_out_ref):
    sums = (part0_ref[...] + part2_ref[...]) + (part1_ref[...] + part3_ref[...])
    length = scalars_ref[0:1, 0:1] / (total(sums) + damping * scalars_ref[8:9, 0:1])
    solution = solution_ref[...] + length * direction_ref[...]
    density_out_ref[...] = to_rows(density_ref[...] + depth_ref[...] * solution)
    misfit_out_ref[...] = misfit_ref[...] - (change_ref[...] + length * share_ref[...])


def shifts_along_rows(values):
    n = lax.axis_size("rows")
    opposite, left, right = (
        lax.ppermute(values, "rows", [(i, (i + step) % n) for i in range(n)]) for step in (2, 1, 3)
    )
    return values, left, opposite, right


def exchange(message):
    own = lax.all_to_all(message, ("x", "z"), 0, 0)
    return own, lax.ppermute(own, "core", [(0, 1), (1, 0)])


def call(kernel, out_shape, operands, scratch=()):
    spaces = [
        pltpu.VMEM if jnp.issubdtype(a.dtype, jnp.floating) else pltpu.SMEM for a in operands
    ]
    return pl.pallas_call(
        kernel,
        out_shape=out_shape,
        in_specs=[pl.BlockSpec(memory_space=space) for space in spaces],
        out_specs=jax.tree.map(lambda _: pl.BlockSpec(memory_space=pltpu.VMEM), out_shape),
        scratch_shapes=list(scratch),
        compiler_params=pltpu.CompilerParams(vmem_limit_bytes=24 * 2**20),
    )(*operands)


def first_sums(tiles, slot_rows, slot_cols, slot_kept, misfit, data_weight):
    weighted = (data_weight * data_weight * misfit).astype(jnp.bfloat16).reshape(-1, TILE)
    blocks = jnp.arange(weighted.shape[0], dtype=jnp.int32)
    picked = jnp.dot(
        (slot_rows[:, None] == blocks[None, :]).astype(jnp.bfloat16),
        weighted,
        preferred_element_type=jnp.float32,
    ).astype(jnp.bfloat16)
    products = jnp.einsum("sab,sa->sb", tiles, picked, preferred_element_type=jnp.float32)
    live = jnp.arange(TILE, dtype=jnp.int32)[None, :] < slot_kept[:, None]
    products = jnp.where(live, products, 0.0)
    pick_cols = slot_cols[None, :] == jnp.arange(2, dtype=jnp.int32)[:, None]
    return jnp.dot(pick_cols.astype(jnp.float32), products, precision=lax.Precision.HIGHEST)


def per_device(
    sensitivity, tile_rows, tile_cols, kept_counts, misfit, data_weight, depth_weight, density
):
    tiles = sensitivity[0]
    signs = haar_signs(TILE)
    turned, analysis = call(
        turn_kernel,
        tuple(jax.ShapeDtypeStruct(a.shape, a.dtype) for a in (tiles, signs)),
        (tiles, signs),
    )
    slots = jnp.concatenate([tile_rows, tile_cols, kept_counts], axis=1)
    depth, density = (a.reshape(2, TILE) for a in (depth_weight, density))
    own_misfit = lax.dynamic_slice_in_dim(misfit.reshape(-1, LANES), my_column() * 8, 8)
    planes = lax.axis_size("x") * lax.axis_size("z")
    f32 = functools.partial(jax.ShapeDtypeStruct, dtype=jnp.float32)
    cells, rows, parts = f32((2, TILE)), f32((8, LANES)), f32((2, TILE + LANES))
    scalars_shape, field_shape = f32((16, LANES)), f32((2 * LANES, 2 * LANES))
    message_shapes = [
        jax.ShapeDtypeStruct(
            (planes, MESSAGE_ROWS + (PRODUCT_ROWS if n in FINE else 0), LANES), jnp.bfloat16
        )
        for n in range(ITERS)
    ]
    pick_shape = jax.ShapeDtypeStruct((16, 2 * LANES), jnp.bfloat16)

    masks, row_ids, pick, squared = call(
        prepare_kernel,
        (f32((8, TILE)), rows, pick_shape, field_shape),
        (slots, data_weight.reshape(-1, LANES)),
    )
    part = first_sums(tiles, tile_rows[0], tile_cols[0], kept_counts[0], misfit, data_weight)
    message, residual = call(
        first_forward_kernel,
        (message_shapes[0], cells),
        (masks, row_ids, tiles, signs, depth, density) + shifts_along_rows(part),
    )
    part, scalars, share, field, ids = call(
        first_data_kernel,
        (parts, scalars_shape, rows, field_shape, f32((8, planes * 8))),
        (masks, pick, tiles, squared) + exchange(message),
    )
    direction = residual
    sofar = ()
    for iteration in range(1, ITERS):
        message, residual, *sofar = call(
            functools.partial(step_kernel, iteration > 1),
            (message_shapes[iteration], cells, cells, rows),
            (masks, row_ids, turned, signs, analysis, depth, residual, direction, scalars, share)
            + (*sofar, *shifts_along_rows(part)),
        )
        carried = (squared, residual, direction, scalars, field, ids) + exchange(message)
        if iteration + 1 < ITERS:
            part, direction, scalars, share, field = call(
                data_kernel,
                (parts, cells, scalars_shape, rows, field_shape),
                (masks, pick, tiles) + carried,
            )
    part, direction, scalars, share = call(
        last_data_kernel,
        (f32((2, LANES)), cells, scalars_shape, rows),
        carried,
        [pltpu.VMEM(field_shape.shape, jnp.float32)],
    )
    new_density, new_misfit = call(
        last_kernel,
        (rows, rows),
        (depth, density, own_misfit, direction, scalars, share, *sofar) + shifts_along_rows(part),
    )
    return (new_density.reshape(-1), new_misfit.reshape(-1))


def solution(mesh):
    cols = ("x", "z", "core")
    fine = Mesh(mesh.devices.reshape(4, 4, 8, 2), ("rows",) + cols)
    return jax.shard_map(
        per_device,
        mesh=fine,
        in_specs=(
            P("rows", cols, None, None),
            P("rows", cols),
            P("rows", cols),
            P("rows", cols),
            P("rows"),
            P("rows"),
            P(cols),
            P(cols),
        ),
        out_specs=(P(cols), P(("rows",) + cols)),
        check_vma=False,
    )
```
